32 devices in a mesh: grp: 2 (over x), patch: 4 (over y, core), wring: 4 (over z).
Axes of the slice: x: 2, y: 2, z: 4, core: 2. Of those that a mesh axis runs over, the one named last changes fastest.
Arguments:
- tokens: bfloat16 [4096, 6144], P(('grp', 'patch', 'wring')), parts along dimension 0, may hold values from -6 to 6
- mod_scale: float32 [6144], replicated, may hold values from -1.5 to 1.5
- mod_shift: float32 [6144], replicated, may hold values from -1.5 to 1.5
- q_weight: bfloat16 [6144, 3072], P(None, 'wring'), may hold values from -0.078125 to 0.078125
- q_gain: float32 [3072], P('wring'), may hold values from 1.5 to 3
- stale_keys: bfloat16 [4096, 3072], P(('grp', 'patch'), 'wring'), parts along dimension 0, may hold values from -6 to 6
- stale_values: bfloat16 [4096, 3072], P(('grp', 'patch'), 'wring'), parts along dimension 0, may hold values from -12 to 12
- kv_lists: int32 [8, 4, 1], P('grp'), parts along dimension 0, may hold values from -1 to 3, as said below
- block_mask: int32 [32, 16], P('grp'), parts along dimension 0, may hold values from 0 to 1, as said below
Outputs:
- attended: bfloat16 [4096, 3072], P(('grp', 'patch'), 'wring'), parts along dimension 0
The draws below stay inside these ranges and needn't reach their ends.
There are 2 independent parts, one for each index of `grp`. The reference program is written for one: setup_inputs(seed, part) draws one part's arguments, and reference() takes and returns one part's arrays. A program takes and returns all parts, laid end to end along the dimension named above; an argument that names none is the same for every part. Nothing has to cross between parts.
Inputs may be any that keep to these rules, and one draw needn't show every extreme that they name: kv_lists[d, s, j] holds distinct block numbers within patch s in its first slots and -1 after them; all slots are -1 when d == s; each pair lists at most 1 block, and in every draw one patch reads 1 block from every other patch. block_mask[a, a] is 1; block_mask[a, b] is 1 for a block b of another patch only where b is listed for the two patches in kv_lists; every listed block is attended by some query block of the reading patch.
All inputs are finite; a program needn't handle non-finite values.
Results may differ from the reference program's by a relative error of at most 0.012.
Values may be sent and summed in bfloat16 or wider, within the bound.
A program may use at most 128 MiB of HBM per device.

```python
import math
import jax
import jax.numpy as jnp
from jax import lax

D = 6144
DH = 128
H = 24
BLK = 128
MAXB = 1
HD = 3072
P_TOK = 512
BP = 4
NB = 16
TOKENS = 2048
N_PATCH = 4


def kv_plan(key):
    key_busiest, key_count, key_ranking, key_chosen, key_bits = jax.random.split(key, 5)
    busiest = jax.random.randint(key_busiest, (), 0, N_PATCH)
    counts = jax.random.randint(key_count, (N_PATCH, N_PATCH), 0, MAXB + 1)
    row_index = jnp.arange(N_PATCH, dtype=jnp.int32)[:, None]
    col_index = jnp.arange(N_PATCH, dtype=jnp.int32)[None, :]
    counts = jnp.where(row_index == busiest, MAXB, counts)
    counts = jnp.where(row_index == col_index, 0, counts)
    ranking = jax.random.randint(key_ranking, (N_PATCH, N_PATCH, BP), 0, 1 << 20) * BP + jnp.arange(BP, dtype=jnp.int32)
    ordered = jnp.argsort(ranking, axis=-1, stable=True)[..., :MAXB].astype(jnp.int32)
    slot_number = jnp.arange(MAXB, dtype=jnp.int32)
    patch_lists = jnp.where(slot_number < counts[..., None], ordered, -1).astype(jnp.int32)
    listed = jnp.any(patch_lists[..., None] == jnp.arange(BP, dtype=jnp.int32), axis=2)
    same_patch = (row_index == col_index)[:, None, :, None]
    allowed = jnp.logical_or(same_patch, listed[:, None, :, :])
    allowed = jnp.broadcast_to(allowed, (N_PATCH, BP, N_PATCH, BP))
    random_bits = jax.random.randint(key_bits, (N_PATCH, BP, N_PATCH, BP), 0, 2) == 1
    chosen_row = jax.random.randint(key_chosen, (N_PATCH, N_PATCH, BP), 0, BP)
    forced = jnp.logical_and(jnp.arange(BP, dtype=jnp.int32)[None, :, None, None] == chosen_row[:, None, :, :], listed[:, None, :, :])
    pattern = jnp.logical_or(jnp.logical_and(allowed, random_bits), forced).reshape(NB, NB)
    pattern = jnp.logical_or(pattern, jnp.eye(NB, dtype=bool))
    return (patch_lists, pattern.astype(jnp.int32))


def draw_kv_lists(key, part):
    patch_lists, pattern = kv_plan(key)
    return patch_lists


def draw_block_mask(key, part):
    patch_lists, pattern = kv_plan(key)
    return pattern


def block_scale(key, extent, cuts, low, top_value):
    def one(axis_at, parts):
        steps = jax.random.uniform(jax.random.fold_in(jax.random.fold_in(key, 6), axis_at), (parts,), jnp.float32, low / len(cuts), top_value / len(cuts))
        return jnp.repeat(jnp.exp(steps), extent[axis_at] // parts).reshape((-1,) + (1,) * (len(extent) - axis_at - 1))

    level = one(*cuts[0])
    for cut in cuts[1:]:
        level = level * one(*cut)
    return level


def scatter_about(stream_key, dims, scale, reach, cuts=(), kind=jnp.bfloat16):
    values = scale * jax.random.normal(stream_key, dims, jnp.float32)
    if cuts:
        values = values * block_scale(stream_key, dims, cuts, -0.22, 0.18)
    return jnp.clip(values, -reach, reach).astype(kind)


def setup_inputs(seed: int = 0, part: int = 0) -> dict:
    keys = jax.random.split(jax.random.key(seed), 10)
    own_keys = jax.random.split(jax.random.fold_in(keys[9], part), 10)
    tokens = scatter_about(own_keys[0], (TOKENS, D), 1.0, 6.0, ((0, 16),))
    mod_scale = scatter_about(keys[1], (D,), 0.3, 1.5, (), jnp.float32)
    mod_shift = scatter_about(keys[2], (D,), 0.3, 1.5, (), jnp.float32)
    q_weight = scatter_about(keys[3], (D, HD), D ** -0.5, 0.078125, ((1, 4),))
    q_gain = jnp.clip(1.5 + 1.5 * jax.random.uniform(keys[4], (HD,), jnp.float32) ** block_scale(keys[4], (HD,), ((0, 4),), -0.2, 0.2), 1.5, 3.0)
    stale_keys = scatter_about(own_keys[5], (TOKENS, HD), 1.0, 6.0, ((0, 4), (1, 4)))
    stale_values = scatter_about(own_keys[6], (TOKENS, HD), 2.0, 12.0, ((0, 4), (1, 4)))
    kv_lists = draw_kv_lists(jax.random.fold_in(jax.random.fold_in(keys[9], part), 71), part)
    block_mask = draw_block_mask(jax.random.fold_in(jax.random.fold_in(keys[9], part), 71), part)
    return dict(tokens=tokens, mod_scale=mod_scale, mod_shift=mod_shift, q_weight=q_weight, q_gain=q_gain, stale_keys=stale_keys, stale_values=stale_values, kv_lists=kv_lists, block_mask=block_mask)


def rms_rows(values):
    return values * lax.rsqrt(lax.optimization_barrier(jnp.mean(values * values, axis=-1, keepdims=True)) + 1e-06)

def reference(tokens, mod_scale, mod_shift, q_weight, q_gain, stale_keys, stale_values, kv_lists, block_mask):
    floats = tokens.astype(jnp.float32)
    centre = lax.optimization_barrier(jnp.mean(floats, axis=-1, keepdims=True))
    spread = lax.optimization_barrier(jnp.mean((floats - centre) * (floats - centre), axis=-1, keepdims=True))
    normed = ((floats - centre) * lax.rsqrt(spread + 1e-06) * (1.0 + mod_scale) + mod_shift).astype(jnp.bfloat16)
    queries = jnp.dot(normed, q_weight, preferred_element_type=jnp.float32).astype(jnp.bfloat16)
    q_hat = (rms_rows(queries.astype(jnp.float32).reshape(TOKENS, H, DH)) * q_gain.reshape(H, DH)).astype(jnp.bfloat16)
    k_hat = rms_rows(stale_keys.astype(jnp.float32).reshape(TOKENS, H, DH)).astype(jnp.bfloat16)
    q_tiles = q_hat.reshape(N_PATCH, P_TOK, H, DH)
    k_blocks = k_hat.reshape(NB, BLK, H, DH)
    v_blocks = stale_values.reshape(NB, BLK, H, DH)
    inverse_root = 1.0 / math.sqrt(DH)

    def attend_patch(patch_index):
        patch_lists = kv_lists[patch_index]
        slot_live = (patch_lists >= 0).reshape(-1)
        remote = (jnp.arange(N_PATCH, dtype=jnp.int32)[:, None] * BP + jnp.maximum(patch_lists, 0)).reshape(-1)
        block_ids = jnp.concatenate([patch_index * BP + jnp.arange(BP, dtype=jnp.int32), remote.astype(jnp.int32)])
        usable = jnp.concatenate([jnp.ones((BP,), jnp.float32), slot_live.astype(jnp.float32)])
        mask_rows = lax.dynamic_slice_in_dim(block_mask, (patch_index * BP).astype(jnp.int32), BP, 0)
        allowed = mask_rows[:, block_ids].astype(jnp.float32) * usable[None, :]
        key_rows = jnp.transpose(k_blocks[block_ids].reshape(-1, H, DH), (1, 0, 2))
        value_rows = jnp.transpose(v_blocks[block_ids].reshape(-1, H, DH), (1, 0, 2))
        query_rows = jnp.transpose(lax.dynamic_index_in_dim(q_tiles, patch_index, 0, keepdims=False), (1, 0, 2))

        def attend_head(operands):
            query_head, key_head, value_head = operands
            scores = jnp.dot(query_head, key_head.T, preferred_element_type=jnp.float32)
            weights = jnp.exp(scores * inverse_root).reshape(BP, BLK, -1, BLK) * allowed[:, None, :, None]
            weights = weights.reshape(P_TOK, -1)
            shares = (weights / lax.optimization_barrier(jnp.sum(weights, axis=1, keepdims=True))).astype(jnp.bfloat16)
            return jnp.dot(shares, value_head, preferred_element_type=jnp.float32).astype(jnp.bfloat16)
        per_head = lax.map(attend_head, (query_rows, key_rows, value_rows))
        return jnp.transpose(per_head, (1, 0, 2)).reshape(P_TOK, HD)
    results = lax.map(attend_patch, jnp.arange(N_PATCH, dtype=jnp.int32))
    return results.reshape(TOKENS, HD)
```

```python
import functools
import math

import jax
import jax.numpy as jnp
from jax import lax
from jax.experimental import pallas as pl
from jax.experimental.pallas import tpu as pltpu
from jax.sharding import PartitionSpec as P

DH = 128
BLK = 128
CHUNKS = 8
F32 = jnp.float32
BF16 = jnp.bfloat16
SCORE_SCALE = math.log2(math.e) / math.sqrt(DH)


def rms_rows(values):
    return values * lax.rsqrt(jnp.mean(values * values, axis=-1, keepdims=True) + 1e-06)


def body(
    n, patches, slots,
    tok, scale, shift, w_hbm, gain, k_hbm, v_hbm, lists, mask, out,
    held, w, acc, qh, kraw, vall, khat, sendkv,
    w_sem, kv_sem, send_sem, recv_sem, kvs_sem, kvr_sem,
):
    me = lax.axis_index("wring")
    mp = lax.axis_index("patch")
    rows = tok.shape[0]
    width = tok.shape[1]
    kc = width // CHUNKS
    heads = gain.shape[1] // DH
    local = k_hbm.shape[0]
    bp = local // BLK

    w_copy = pltpu.make_async_copy(w_hbm, w, w_sem)
    w_copy.start()
    k_copy = pltpu.make_async_copy(k_hbm, kraw.at[pl.ds(0, local)], kv_sem.at[0])
    v_copy = pltpu.make_async_copy(v_hbm, vall.at[pl.ds(0, local)], kv_sem.at[1])
    k_copy.start()
    v_copy.start()

    barrier = pltpu.get_barrier_semaphore()

    @pl.when(me > 0)
    def _():
        pl.semaphore_signal(barrier, inc=1, device_id={"wring": me - 1})

    @pl.when(me < n - 1)
    def _():
        pl.semaphore_signal(barrier, inc=1, device_id={"wring": me + 1})

    for o in range(1, patches):
        pl.semaphore_signal(barrier, inc=1, device_id={"patch": lax.rem(mp + o, patches)})

    step = 16

    def norm_rows(i, carry):
        at = pl.ds(pl.multiple_of(i * step, step), step)
        x = tok[at, :].astype(F32)
        centred = x - jnp.mean(x, axis=-1, keepdims=True)
        spread = jnp.mean(centred * centred, axis=-1, keepdims=True)
        y = centred * lax.rsqrt(spread + 1e-06) * (1.0 + scale[...]) + shift[...]
        y = y.astype(BF16)
        for c in range(CHUNKS):
            held[me, c, at, :] = y[:, c * kc : (c + 1) * kc]
        return carry

    lax.fori_loop(0, rows // step, norm_rows, 0)

    edges = jnp.where(me > 0, 1, 0) + jnp.where(me < n - 1, 1, 0)
    pl.semaphore_wait(barrier, edges + patches - 1)

    def hop(shard, c, way):
        return pltpu.make_async_remote_copy(
            src_ref=held.at[shard, c],
            dst_ref=held.at[shard, c],
            send_sem=send_sem.at[way, shard, c],
            recv_sem=recv_sem.at[shard, c],
            device_id={"wring": me - 1 if way == 0 else me + 1},
        )

    def each(fn):
        def one(c, carry):
            fn(c)
            return carry

        lax.fori_loop(0, CHUNKS, one, 0)

    def send_own(c):
        @pl.when(me > 0)
        def _():
            hop(me, c, 0).start()

        @pl.when(me < n - 1)
        def _():
            hop(me, c, 1).start()

    each(send_own)

    k_copy.wait()
    v_copy.wait()

    def kv_copy(o, j, which):
        slot = (o - 1) * slots + j
        return pltpu.make_async_remote_copy(
            src_ref=sendkv.at[slot, which],
            dst_ref=(kraw, vall)[which].at[pl.ds(local + slot * BLK, BLK)],
            send_sem=kvs_sem.at[slot, which],
            recv_sem=kvr_sem.at[slot, which],
            device_id={"patch": lax.rem(mp + o, patches)},
        )

    pairs = [(o, j) for o in range(1, patches) for j in range(slots)]
    for o, j in pairs:
        slot = (o - 1) * slots + j
        picked = jnp.maximum(lists[lax.rem(mp + o, patches), mp, j], 0)
        for which, blocks in enumerate((kraw, vall)):
            chosen = jnp.zeros((BLK, sendkv.shape[3]), F32)
            for b in range(bp):
                chosen = chosen + blocks[b * BLK : (b + 1) * BLK, :].astype(F32) * (
                    jnp.where(picked == b, 1, 0).astype(F32)
                )
            sendkv[slot, which] = chosen.astype(BF16)
        kv_copy(o, j, 0).start()
        kv_copy(o, j, 1).start()

    w_copy.wait()

    def project(shard, c, way):
        part = jnp.dot(
            held[shard, c],
            w[pl.ds(pl.multiple_of(c * kc, kc), kc), :],
            preferred_element_type=F32,
        )

        @pl.when(c == 0)
        def _():
            acc[way] = part

        @pl.when(c > 0)
        def _():
            acc[way] = acc[way] + part

    each(lambda c: project(me, c, 0))

    for o, j in pairs:
        for which in range(2):
            kv_copy(o, j, which).wait_recv()
            kv_copy(o, j, which).wait_send()

    def norm_keys(i, carry):
        at = pl.ds(pl.multiple_of(i * BLK, BLK), BLK)
        for h in range(heads):
            lanes = slice(h * DH, (h + 1) * DH)
            khat[at, lanes] = rms_rows(kraw[at, lanes].astype(F32)).astype(BF16)
        return carry

    lax.fori_loop(0, khat.shape[0] // BLK, norm_keys, 0)

    def attend(shard, way):
        for h in range(heads):
            lanes = slice(h * DH, (h + 1) * DH)
            q = acc[way, :, lanes].astype(BF16).astype(F32)
            qh[:, lanes] = (rms_rows(q) * gain[:, lanes]).astype(BF16)
        for a in range(rows // BLK):
            row = mp * bp + shard * (rows // BLK) + a
            flags = [mask[row, mp * bp + b] for b in range(bp)]
            for o, j in pairs:
                owner = lax.rem(mp + patches - o, patches)
                listed = lists[mp, owner, j]
                flag = 0
                for b in range(bp):
                    flag = flag + jnp.where(listed == b, mask[row, owner * bp + b], 0)
                flags.append(flag)
            allowed = jnp.concatenate(
                [jnp.full((1, BLK), flag.astype(F32), F32) for flag in flags], axis=1
            )
            here = pl.ds(a * BLK, BLK)
            there = pl.ds(pl.multiple_of(shard * rows + a * BLK, BLK), BLK)

            def one_head(h, carry):
                lanes = pl.ds(pl.multiple_of(h * DH, DH), DH)
                scores = lax.dot_general(
                    qh[here, lanes], khat[:, lanes], (((1,), (1,)), ((), ())),
                    preferred_element_type=F32,
                )
                weights = (jnp.exp2(scores * SCORE_SCALE) * allowed).astype(BF16)
                values = vall[:, lanes]
                wide = jnp.concatenate([values, jnp.ones_like(values)], axis=1)
                both = jnp.dot(weights, wide, preferred_element_type=F32)
                out[there, lanes] = (both[:, :DH] / both[:, DH:]).astype(BF16)
                return carry

            lax.fori_loop(0, heads, one_head, 0)

    attend(me, 0)

    for h in range(1, n):
        def take(c, h=h):
            for way, shard in ((1, me - h), (0, me + h)):
                @pl.when((shard >= 0) & (shard < n))
                def _(way=way, shard=shard):
                    hop(shard, c, way).wait_recv()

                    @pl.when((me < n - 1) if way == 1 else (me > 0))
                    def _():
                        hop(shard, c, way).start()

                    project(shard, c, way)

        each(take)
        for way, shard in ((1, me - h), (0, me + h)):
            @pl.when((shard >= 0) & (shard < n))
            def _(way=way, shard=shard):
                attend(shard, way)

    for h in range(n):
        for way, shard in ((1, me - h), (0, me + h)):
            @pl.when(
                (shard >= 0) & (shard < n) & ((me < n - 1) if way == 1 else (me > 0))
            )
            def _(way=way, shard=shard):
                each(lambda c: hop(shard, c, way).wait_send())


def on_device(
    n, patches, tokens, mod_scale, mod_shift, q_weight, q_gain, stale_keys, stale_values,
    kv_lists, block_mask
):
    rows, width = tokens.shape
    cols = q_weight.shape[1]
    local = stale_keys.shape[0]
    slots = kv_lists.shape[2]
    got = (patches - 1) * slots
    keys = local + got * BLK
    vmem = pl.BlockSpec(memory_space=pltpu.VMEM)
    smem = pl.BlockSpec(memory_space=pltpu.SMEM)
    hbm = pl.BlockSpec(memory_space=pl.ANY)
    dma = pltpu.SemaphoreType.DMA
    return pl.pallas_call(
        functools.partial(body, n, patches, slots),
        out_shape=jax.ShapeDtypeStruct((local, cols), BF16),
        in_specs=[vmem, vmem, vmem, hbm, vmem, hbm, hbm, smem, smem],
        out_specs=vmem,
        scratch_shapes=[
            pltpu.VMEM((n, CHUNKS, rows, width // CHUNKS), BF16),
            pltpu.VMEM((width, cols), BF16),
            pltpu.VMEM((2, rows, cols), F32),
            pltpu.VMEM((rows, cols), BF16),
            pltpu.VMEM((keys, cols), BF16),
            pltpu.VMEM((keys, cols), BF16),
            pltpu.VMEM((keys, cols), BF16),
            pltpu.VMEM((got, 2, BLK, cols), BF16),
            dma,
            dma((2,)),
            dma((2, n, CHUNKS)),
            dma((n, CHUNKS)),
            dma((got, 2)),
            dma((got, 2)),
        ],
        compiler_params=pltpu.CompilerParams(
            collective_id=0, has_side_effects=True, vmem_limit_bytes=56 * 1024 * 1024
        ),
    )(
        tokens, mod_scale[None], mod_shift[None], q_weight, q_gain[None], stale_keys,
        stale_values, kv_lists, block_mask,
    )


def solution(mesh):
    placed = (
        P(("grp", "patch", "wring"), None),
        P(),
        P(),
        P(None, "wring"),
        P("wring"),
        P(("grp", "patch"), "wring"),
        P(("grp", "patch"), "wring"),
        P("grp", None, None),
        P("grp", None),
    )
    return jax.shard_map(
        functools.partial(on_device, mesh.shape["wring"], mesh.shape["patch"]),
        mesh=mesh,
        in_specs=placed,
        out_specs=P(("grp", "patch"), "wring"),
        check_vma=False,
    )
```

```python
import functools
import math

import jax
import jax.numpy as jnp
from jax import lax
from jax.experimental import pallas as pl
from jax.experimental.pallas import tpu as pltpu
from jax.sharding import PartitionSpec as P

DH = 128
BLK = 128
CHUNKS = 8
F32 = jnp.float32
BF16 = jnp.bfloat16
SCORE_SCALE = math.log2(math.e) / math.sqrt(DH)


def rms_rows(values):
    return values * lax.rsqrt(jnp.mean(values * values, axis=-1, keepdims=True) + 1e-06)


def body(
    n, patches, slots,
    tok, scale, shift, w_hbm, gain, k_hbm, v_hbm, lists, mask, out,
    held, w, acc, qh, kraw, vall, khat, sendkv,
    w_sem, kv_sem, send_sem, recv_sem, kvs_sem, kvr_sem,
):
    me = lax.axis_index("wring")
    mp = lax.axis_index("patch")
    rows = tok.shape[0]
    width = tok.shape[1]
    kc = width // CHUNKS
    heads = gain.shape[1] // DH
    local = k_hbm.shape[0]
    bp = local // BLK

    w_copy = pltpu.make_async_copy(w_hbm, w, w_sem)
    w_copy.start()
    k_copy = pltpu.make_async_copy(k_hbm, kraw.at[pl.ds(0, local)], kv_sem.at[0])
    v_copy = pltpu.make_async_copy(v_hbm, vall.at[pl.ds(0, local)], kv_sem.at[1])
    k_copy.start()
    v_copy.start()

    barrier = pltpu.get_barrier_semaphore()

    @pl.when(me > 0)
    def _():
        pl.semaphore_signal(barrier, inc=1, device_id={"wring": me - 1})

    @pl.when(me < n - 1)
    def _():
        pl.semaphore_signal(barrier, inc=1, device_id={"wring": me + 1})

    for o in range(1, patches):
        pl.semaphore_signal(barrier, inc=1, device_id={"patch": lax.rem(mp + o, patches)})

    step = 16

    def norm_rows(i, carry):
        at = pl.ds(pl.multiple_of(i * step, step), step)
        x = tok[at, :].astype(F32)
        centred = x - jnp.mean(x, axis=-1, keepdims=True)
        spread = jnp.mean(centred * centred, axis=-1, keepdims=True)
        y = centred * lax.rsqrt(spread + 1e-06) * (1.0 + scale[...]) + shift[...]
        y = y.astype(BF16)
        for c in range(CHUNKS):
            held[me, c, at, :] = y[:, c * kc : (c + 1) * kc]
        return carry

    lax.fori_loop(0, rows // step, norm_rows, 0)

    edges = jnp.where(me > 0, 1, 0) + jnp.where(me < n - 1, 1, 0)
    pl.semaphore_wait(barrier, edges + patches - 1)

    def hop(shard, c, way):
        return pltpu.make_async_remote_copy(
            src_ref=held.at[shard, c],
            dst_ref=held.at[shard, c],
            send_sem=send_sem.at[way, shard, c],
            recv_sem=recv_sem.at[shard, c],
            device_id={"wring": me - 1 if way == 0 else me + 1},
        )

    def each(fn):
        def one(c, carry):
            fn(c)
            return carry

        lax.fori_loop(0, CHUNKS, one, 0)

    def send_own(c):
        @pl.when(me > 0)
        def _():
            hop(me, c, 0).start()

        @pl.when(me < n - 1)
        def _():
            hop(me, c, 1).start()

    each(send_own)

    k_copy.wait()
    v_copy.wait()

    def kv_copy(o, j, which):
        slot = (o - 1) * slots + j
        return pltpu.make_async_remote_copy(
            src_ref=sendkv.at[slot, which],
            dst_ref=(kraw, vall)[which].at[pl.ds(local + slot * BLK, BLK)],
            send_sem=kvs_sem.at[slot, which],
            recv_sem=kvr_sem.at[slot, which],
            device_id={"patch": lax.rem(mp + o, patches)},
        )

    pairs = [(o, j) for o in range(1, patches) for j in range(slots)]
    for o, j in pairs:
        slot = (o - 1) * slots + j
        picked = jnp.maximum(lists[lax.rem(mp + o, patches), mp, j], 0)
        for which, blocks in enumerate((kraw, vall)):
            chosen = jnp.zeros((BLK, sendkv.shape[3]), F32)
            for b in range(bp):
                chosen = chosen + blocks[b * BLK : (b + 1) * BLK, :].astype(F32) * (
                    jnp.where(picked == b, 1, 0).astype(F32)
                )
            sendkv[slot, which] = chosen.astype(BF16)
        kv_copy(o, j, 0).start()
        kv_copy(o, j, 1).start()

    w_copy.wait()

    def project(shard, c, way):
        part = jnp.dot(
            held[shard, c],
            w[pl.ds(pl.multiple_of(c * kc, kc), kc), :],
            preferred_element_type=F32,
        )

        @pl.when(c == 0)
        def _():
            acc[way] = part

        @pl.when(c > 0)
        def _():
            acc[way] = acc[way] + part

    each(lambda c: project(me, c, 0))

    for o, j in pairs:
        for which in range(2):
            kv_copy(o, j, which).wait_recv()
            kv_copy(o, j, which).wait_send()

    def norm_keys(i, carry):
        at = pl.ds(pl.multiple_of(i * BLK, BLK), BLK)
        for h in range(heads):
            lanes = slice(h * DH, (h + 1) * DH)
            khat[at, lanes] = rms_rows(kraw[at, lanes].astype(F32)).astype(BF16)
        return carry

    lax.fori_loop(0, khat.shape[0] // BLK, norm_keys, 0)

    def attend(shard, way):
        for h in range(heads):
            lanes = slice(h * DH, (h + 1) * DH)
            q = acc[way, :, lanes].astype(BF16).astype(F32)
            qh[:, lanes] = (rms_rows(q) * gain[:, lanes]).astype(BF16)
        for a in range(rows // BLK):
            row = mp * bp + shard * (rows // BLK) + a
            flags = [mask[row, mp * bp + b] for b in range(bp)]
            for o, j in pairs:
                owner = lax.rem(mp + patches - o, patches)
                listed = lists[mp, owner, j]
                flag = 0
                for b in range(bp):
                    flag = flag + jnp.where(listed == b, mask[row, owner * bp + b], 0)
                flags.append(flag)
            allowed = jnp.concatenate(
                [jnp.full((1, BLK), flag.astype(F32), F32) for flag in flags], axis=1
            )
            here = pl.ds(a * BLK, BLK)
            there = pl.ds(pl.multiple_of(shard * rows + a * BLK, BLK), BLK)

            def one_head(h, carry):
                lanes = pl.ds(pl.multiple_of(h * DH, DH), DH)
                scores = lax.dot_general(
                    qh[here, lanes], khat[:, lanes], (((1,), (1,)), ((), ())),
                    preferred_element_type=F32,
                )
                weights = (jnp.exp2(scores * SCORE_SCALE) * allowed).astype(BF16)
                values = vall[:, lanes]
                wide = jnp.concatenate([values, jnp.ones_like(values)], axis=1)
                both = jnp.dot(weights, wide, preferred_element_type=F32)
                out[there, lanes] = (both[:, :DH] / both[:, DH:]).astype(BF16)
                return carry

            lax.fori_loop(0, heads, one_head, 0)

    attend(me, 0)

    for h in range(1, n):
        def take(c, h=h):
            for way, shard in ((1, me - h), (0, me + h)):
                @pl.when((shard >= 0) & (shard < n))
                def _(way=way, shard=shard):
                    hop(shard, c, way).wait_recv()

                    @pl.when((me < n - 1) if way == 1 else (me > 0))
                    def _():
                        hop(shard, c, way).start()

                    project(shard, c, way)

        each(take)
        for way, shard in ((1, me - h), (0, me + h)):
            @pl.when((shard >= 0) & (shard < n))
            def _(way=way, shard=shard):
                attend(shard, way)

    for h in range(n):
        for way, shard in ((1, me - h), (0, me + h)):
            @pl.when(
                (shard >= 0) & (shard < n) & ((me < n - 1) if way == 1 else (me > 0))
            )
            def _(way=way, shard=shard):
                each(lambda c: hop(shard, c, way).wait_send())


def body_assisted(
    patches, slots,
    tok, scale, shift, w_hbm, gain, k_hbm, v_hbm, lists, mask, out,
    held, w, w2, acc, qh, qout, qin, kraw, vall, khat, sendkv,
    w_sem, kv_sem, send_sem, recv_sem, ws_sem, wr_sem, qs_sem, qr_sem, kvs_sem, kvr_sem,
):
    me = lax.axis_index("wring")
    mp = lax.axis_index("patch")
    mg = lax.axis_index("grp")
    inner = (me == 1) | (me == 2)
    end = (me == 0) | (me == 3)
    partner = me + 1 - 2 * lax.rem(me, 2)
    cross = 3 - me
    far = 3 - partner
    core = lax.rem(mp, 2)
    side = mp // 2
    rows = tok.shape[0]
    width = tok.shape[1]
    kc = width // CHUNKS
    piece = kc // 8
    heads = gain.shape[1] // DH
    local = k_hbm.shape[0]
    bp = local // BLK

    w_copy = pltpu.make_async_copy(w_hbm, w, w_sem)
    w_copy.start()
    k_copy = pltpu.make_async_copy(k_hbm, kraw.at[pl.ds(0, local)], kv_sem.at[0])
    v_copy = pltpu.make_async_copy(v_hbm, vall.at[pl.ds(0, local)], kv_sem.at[1])
    k_copy.start()
    v_copy.start()

    barrier = pltpu.get_barrier_semaphore()
    pl.semaphore_signal(barrier, inc=1, device_id={"wring": partner})

    @pl.when(inner)
    def _():
        pl.semaphore_signal(barrier, inc=1, device_id={"wring": cross})

    pl.semaphore_signal(barrier, inc=1, device_id={"grp": 1 - mg})
    for o in range(1, patches):
        pl.semaphore_signal(barrier, inc=1, device_id={"patch": lax.rem(mp + o, patches)})
    pl.semaphore_wait(barrier, jnp.where(inner, 1, 0) + 1 + patches)

    def each(fn, count=CHUNKS):
        def one(c, carry):
            fn(c)
            return carry

        lax.fori_loop(0, count, one, 0)

    def spread(stage, c):
        odd = lax.rem(c, 2)
        even = 1 - odd
        first = core * 4
        count = 1
        where = {"wring": partner}
        if stage in (0, 1):
            first = first + even * (side * 2 + mg) + odd * (mg * 2 + side)
        elif stage == 2:
            first = first + even * (side * 2) + odd * (mg * 2)
            count = 2
        else:
            count = 4
        use_grp = even if stage == 1 else odd
        if stage in (1, 2):
            where = {
                "grp": mg + use_grp * (1 - 2 * mg),
                "patch": mp + (1 - use_grp) * (2 - 4 * side),
            }
        elif stage == 3:
            where = {"patch": mp + 1 - 2 * core}
        at = pl.ds(pl.multiple_of(c * kc + first * piece, piece), count * piece)
        return pltpu.make_async_remote_copy(
            src_ref=(w_hbm if stage == 0 else w2).at[at],
            dst_ref=w2.at[at],
            send_sem=ws_sem.at[stage, c],
            recv_sem=wr_sem.at[stage, c],
            device_id=where,
        )

    @pl.when(end)
    def _():
        each(lambda c: spread(0, c).start())

    step = 16

    def norm_rows(i, carry):
        at = pl.ds(pl.multiple_of(i * step, step), step)
        x = tok[at, :].astype(F32)
        centred = x - jnp.mean(x, axis=-1, keepdims=True)
        spread_of = jnp.mean(centred * centred, axis=-1, keepdims=True)
        y = centred * lax.rsqrt(spread_of + 1e-06) * (1.0 + scale[...]) + shift[...]
        y = y.astype(BF16)
        for c in range(CHUNKS):
            held[me, c, at, :] = y[:, c * kc : (c + 1) * kc]
        return carry

    lax.fori_loop(0, rows // step, norm_rows, 0)

    def hop(shard, c, target):
        return pltpu.make_async_remote_copy(
            src_ref=held.at[shard, c],
            dst_ref=held.at[shard, c],
            send_sem=send_sem.at[shard, c],
            recv_sem=recv_sem.at[shard, c],
            device_id={"wring": target},
        )

    onward = jnp.where(inner, cross, partner)
    each(lambda c: hop(me, c, onward).start())

    k_copy.wait()
    v_copy.wait()

    def kv_copy(o, j, which):
        slot = (o - 1) * slots + j
        return pltpu.make_async_remote_copy(
            src_ref=sendkv.at[slot, which],
            dst_ref=(kraw, vall)[which].at[pl.ds(local + slot * BLK, BLK)],
            send_sem=kvs_sem.at[slot, which],
            recv_sem=kvr_sem.at[slot, which],
            device_id={"patch": lax.rem(mp + o, patches)},
        )

    pairs = [(o, j) for o in range(1, patches) for j in range(slots)]
    for o, j in pairs:
        slot = (o - 1) * slots + j
        picked = jnp.maximum(lists[lax.rem(mp + o, patches), mp, j], 0)
        for which, blocks in enumerate((kraw, vall)):
            chosen = jnp.zeros((BLK, sendkv.shape[3]), F32)
            for b in range(bp):
                chosen = chosen + blocks[b * BLK : (b + 1) * BLK, :].astype(F32) * (
                    jnp.where(picked == b, 1, 0).astype(F32)
                )
            sendkv[slot, which] = chosen.astype(BF16)
        kv_copy(o, j, 0).start()
        kv_copy(o, j, 1).start()

    w_copy.wait()

    def add(slot, c, part):
        @pl.when(c == 0)
        def _():
            acc[slot] = part

        @pl.when(c > 0)
        def _():
            acc[slot] = acc[slot] + part

    def project(shard, c, weight, slot):
        at = pl.ds(pl.multiple_of(c * kc, kc), kc)
        add(slot, c, jnp.dot(held[shard, c], weight[at, :], preferred_element_type=F32))

    def project_two(one, two, c, weight, slot):
        at = pl.ds(pl.multiple_of(c * kc, kc), kc)
        both = jnp.concatenate([held[one, c], held[two, c]], axis=0)
        part = jnp.dot(both, weight[at, :], preferred_element_type=F32)
        add(slot, c, part[:rows])
        add(slot + 1, c, part[rows:])

    def finish_keys():
        for o, j in pairs:
            for which in range(2):
                kv_copy(o, j, which).wait_recv()
                kv_copy(o, j, which).wait_send()

        def norm_keys(i, carry):
            at = pl.ds(pl.multiple_of(i * BLK, BLK), BLK)
            for h in range(heads):
                lanes = slice(h * DH, (h + 1) * DH)
                khat[at, lanes] = rms_rows(kraw[at, lanes].astype(F32)).astype(BF16)
            return carry

        lax.fori_loop(0, khat.shape[0] // BLK, norm_keys, 0)

    def norm_queries(read, slot):
        for h in range(heads):
            lanes = slice(h * DH, (h + 1) * DH)
            q = read(lanes).astype(BF16).astype(F32)
            qh[slot, :, lanes] = (rms_rows(q) * gain[:, lanes]).astype(BF16)

    def attend_head(shard, slot, h):
        row = mp * bp + shard
        flags = [mask[row, mp * bp + b] for b in range(bp)]
        for o, j in pairs:
            owner = lax.rem(mp + patches - o, patches)
            listed = lists[mp, owner, j]
            flag = 0
            for b in range(bp):
                flag = flag + jnp.where(listed == b, mask[row, owner * bp + b], 0)
            flags.append(flag)
        allowed = jnp.concatenate(
            [jnp.full((1, BLK), flag.astype(F32), F32) for flag in flags], axis=1
        )
        lanes = pl.ds(pl.multiple_of(h * DH, DH), DH)
        scores = lax.dot_general(
            qh[slot, :, lanes], khat[:, lanes], (((1,), (1,)), ((), ())),
            preferred_element_type=F32,
        )
        weights = (jnp.exp2(scores * SCORE_SCALE) * allowed).astype(BF16)
        values = vall[:, lanes]
        wide = jnp.concatenate([values, jnp.ones_like(values)], axis=1)
        both = jnp.dot(weights, wide, preferred_element_type=F32)
        there = pl.ds(pl.multiple_of(shard * rows, rows), rows)
        out[there, lanes] = (both[:, :DH] / both[:, DH:]).astype(BF16)

    def give(shard):
        return pltpu.make_async_remote_copy(
            src_ref=qout.at[shard],
            dst_ref=qin.at[shard],
            send_sem=qs_sem.at[shard],
            recv_sem=qr_sem.at[shard],
            device_id={"wring": partner},
        )

    @pl.when(inner)
    def _():
        def advance(c):
            @pl.when(c < CHUNKS)
            def _():
                spread(0, c).wait_recv()
                spread(1, c).start()

            @pl.when((c >= 1) & (c <= CHUNKS))
            def _():
                spread(1, c - 1).wait_recv()
                spread(2, c - 1).start()

            @pl.when((c >= 2) & (c <= CHUNKS + 1))
            def _():
                spread(2, c - 2).wait_recv()
                spread(3, c - 2).start()

        def early(c):
            advance(c)
            hop(cross, c, cross).wait_recv()
            project_two(me, cross, c, w, 0)

        each(early)
        finish_keys()
        norm_queries(lambda lanes: acc[0, :, lanes], 0)
        norm_queries(lambda lanes: acc[1, :, lanes], 1)

        def middle(c):
            hop(partner, c, cross).wait_recv()
            hop(partner, c, cross).start()

            @pl.when(c < 2)
            def _():
                advance(c + CHUNKS)

            project(partner, c, w, 2)
            spread(3, c).wait_recv()
            project_two(me, cross, c, w2, 3)

            @pl.when(c < heads)
            def _():
                attend_head(me, 0, c)
                attend_head(cross, 1, c)

        each(middle)
        qout[me] = acc[3].astype(BF16)
        give(me).start()
        qout[cross] = acc[4].astype(BF16)
        give(cross).start()
        norm_queries(lambda lanes: acc[2, :, lanes], 0)
        each(lambda h: attend_head(partner, 0, h), heads)

        def late(c):
            hop(far, c, cross).wait_recv()
            project(far, c, w2, 5)
            project(far, c, w, 2)

        each(late)
        qout[far] = acc[5].astype(BF16)
        give(far).start()
        norm_queries(lambda lanes: acc[2, :, lanes], 0)
        each(lambda h: attend_head(far, 0, h), heads)

        def settle(c):
            hop(me, c, cross).wait_send()
            hop(partner, c, cross).wait_send()
            for stage in (1, 2, 3):
                spread(stage, c).wait_send()

        each(settle)
        for shard in (me, cross, far):
            give(shard).wait_send()

    @pl.when(end)
    def _():
        each(lambda c: project(me, c, w, 0))
        finish_keys()
        norm_queries(lambda lanes: acc[0, :, lanes], 0)
        each(lambda h: attend_head(me, 0, h), heads)

        def settle(c):
            hop(me, c, partner).wait_send()
            spread(0, c).wait_send()

        each(settle)

        for shard in (partner, far, cross):
            give(shard).wait_recv()
            norm_queries(lambda lanes: qin[shard, :, lanes], 0)
            each(lambda h: attend_head(shard, 0, h), heads)


def on_device(
    n, patches, groups, tokens, mod_scale, mod_shift, q_weight, q_gain, stale_keys,
    stale_values, kv_lists, block_mask
):
    rows, width = tokens.shape
    cols = q_weight.shape[1]
    local = stale_keys.shape[0]
    slots = kv_lists.shape[2]
    got = (patches - 1) * slots
    keys = local + got * BLK
    vmem = pl.BlockSpec(memory_space=pltpu.VMEM)
    smem = pl.BlockSpec(memory_space=pltpu.SMEM)
    hbm = pl.BlockSpec(memory_space=pl.ANY)
    dma = pltpu.SemaphoreType.DMA
    assisted = (
        (n, patches, groups) == (4, 4, 2)
        and rows == BLK
        and cols // DH <= CHUNKS
        and width % (CHUNKS * 8 * 16) == 0
    )
    held = pltpu.VMEM((n, CHUNKS, rows, width // CHUNKS), BF16)
    w = pltpu.VMEM((width, cols), BF16)
    by_key = [pltpu.VMEM((keys, cols), BF16)] * 3 + [pltpu.VMEM((got, 2, BLK, cols), BF16)]
    if assisted:
        kernel = functools.partial(body_assisted, patches, slots)
        scratch = [
            held, w, w,
            pltpu.VMEM((6, rows, cols), F32),
            pltpu.VMEM((2, rows, cols), BF16),
            pltpu.VMEM((n, rows, cols), BF16),
            pltpu.VMEM((n, rows, cols), BF16),
            *by_key,
            dma, dma((2,)),
            dma((n, CHUNKS)), dma((n, CHUNKS)),
            dma((4, CHUNKS)), dma((4, CHUNKS)),
            dma((n,)), dma((n,)),
            dma((got, 2)), dma((got, 2)),
        ]
    else:
        kernel = functools.partial(body, n, patches, slots)
        scratch = [
            held, w,
            pltpu.VMEM((2, rows, cols), F32),
            pltpu.VMEM((rows, cols), BF16),
            *by_key,
            dma, dma((2,)),
            dma((2, n, CHUNKS)), dma((n, CHUNKS)),
            dma((got, 2)), dma((got, 2)),
        ]
    return pl.pallas_call(
        kernel,
        out_shape=jax.ShapeDtypeStruct((local, cols), BF16),
        in_specs=[vmem, vmem, vmem, hbm, vmem, hbm, hbm, smem, smem],
        out_specs=vmem,
        scratch_shapes=scratch,
        compiler_params=pltpu.CompilerParams(
            collective_id=0, has_side_effects=True, vmem_limit_bytes=56 * 1024 * 1024
        ),
    )(
        tokens, mod_scale[None], mod_shift[None], q_weight, q_gain[None], stale_keys,
        stale_values, kv_lists, block_mask,
    )


def solution(mesh):
    placed = (
        P(("grp", "patch", "wring"), None),
        P(),
        P(),
        P(None, "wring"),
        P("wring"),
        P(("grp", "patch"), "wring"),
        P(("grp", "patch"), "wring"),
        P("grp", None, None),
        P("grp", None),
    )
    return jax.shard_map(
        functools.partial(on_device, mesh.shape["wring"], mesh.shape["patch"], mesh.shape["grp"]),
        mesh=mesh,
        in_specs=placed,
        out_specs=P(("grp", "patch"), "wring"),
        check_vma=False,
    )
```

```python
import functools
import math

import jax
import jax.numpy as jnp
from jax import lax
from jax.experimental import pallas as pl
from jax.experimental.pallas import tpu as pltpu
from jax.sharding import PartitionSpec as P

DH = 128
BLK = 128
CHUNKS = 8
AHEAD = 3
F32 = jnp.float32
BF16 = jnp.bfloat16
SCORE_SCALE = math.log2(math.e) / math.sqrt(DH)


def rms_rows(values):
    return values * lax.rsqrt(jnp.mean(values * values, axis=-1, keepdims=True) + 1e-06)


def body(
    n, patches, slots,
    tok, scale, shift, w_hbm, gain, k_hbm, v_hbm, lists, mask, out,
    held, w, acc, qh, kraw, vall, khat, sendkv,
    w_sem, kv_sem, send_sem, recv_sem, kvs_sem, kvr_sem,
):
    me = lax.axis_index("wring")
    mp = lax.axis_index("patch")
    rows = tok.shape[0]
    width = tok.shape[1]
    kc = width // CHUNKS
    heads = gain.shape[0] // DH
    local = k_hbm.shape[0]
    bp = local // BLK

    w_copy = pltpu.make_async_copy(w_hbm, w, w_sem)
    w_copy.start()
    k_copy = pltpu.make_async_copy(k_hbm, kraw.at[pl.ds(0, local)], kv_sem.at[0])
    v_copy = pltpu.make_async_copy(v_hbm, vall.at[pl.ds(0, local)], kv_sem.at[1])
    k_copy.start()
    v_copy.start()

    barrier = pltpu.get_barrier_semaphore()

    @pl.when(me > 0)
    def _():
        pl.semaphore_signal(barrier, inc=1, device_id={"wring": me - 1})

    @pl.when(me < n - 1)
    def _():
        pl.semaphore_signal(barrier, inc=1, device_id={"wring": me + 1})

    for o in range(1, patches):
        pl.semaphore_signal(barrier, inc=1, device_id={"patch": lax.rem(mp + o, patches)})

    step = 16

    def norm_rows(i, carry):
        at = pl.ds(pl.multiple_of(i * step, step), step)
        x = tok[at, :].astype(F32)
        centred = x - jnp.mean(x, axis=-1, keepdims=True)
        spread = jnp.mean(centred * centred, axis=-1, keepdims=True)
        y = centred * lax.rsqrt(spread + 1e-06) * (1.0 + scale[...][None]) + shift[...][None]
        y = y.astype(BF16)
        for c in range(CHUNKS):
            held[me, c, at, :] = y[:, c * kc : (c + 1) * kc]
        return carry

    lax.fori_loop(0, rows // step, norm_rows, 0)

    edges = jnp.where(me > 0, 1, 0) + jnp.where(me < n - 1, 1, 0)
    pl.semaphore_wait(barrier, edges + patches - 1)

    def hop(shard, c, way):
        return pltpu.make_async_remote_copy(
            src_ref=held.at[shard, c],
            dst_ref=held.at[shard, c],
            send_sem=send_sem.at[way, shard, c],
            recv_sem=recv_sem.at[shard, c],
            device_id={"wring": me - 1 if way == 0 else me + 1},
        )

    def each(fn):
        def one(c, carry):
            fn(c)
            return carry

        lax.fori_loop(0, CHUNKS, one, 0)

    def send_own(c):
        @pl.when(me > 0)
        def _():
            hop(me, c, 0).start()

        @pl.when(me < n - 1)
        def _():
            hop(me, c, 1).start()

    each(send_own)

    k_copy.wait()
    v_copy.wait()

    def kv_copy(o, j, which):
        slot = (o - 1) * slots + j
        return pltpu.make_async_remote_copy(
            src_ref=sendkv.at[slot, which],
            dst_ref=(kraw, vall)[which].at[pl.ds(local + slot * BLK, BLK)],
            send_sem=kvs_sem.at[slot, which],
            recv_sem=kvr_sem.at[slot, which],
            device_id={"patch": lax.rem(mp + o, patches)},
        )

    pairs = [(o, j) for o in range(1, patches) for j in range(slots)]
    for o, j in pairs:
        slot = (o - 1) * slots + j
        picked = jnp.maximum(lists[lax.rem(mp + o, patches), mp, j], 0)
        for which, blocks in enumerate((kraw, vall)):
            chosen = jnp.zeros((BLK, sendkv.shape[3]), F32)
            for b in range(bp):
                chosen = chosen + blocks[b * BLK : (b + 1) * BLK, :].astype(F32) * (
                    jnp.where(picked == b, 1, 0).astype(F32)
                )
            sendkv[slot, which] = chosen.astype(BF16)
        kv_copy(o, j, 0).start()
        kv_copy(o, j, 1).start()

    w_copy.wait()

    def project(shard, c, way):
        part = jnp.dot(
            held[shard, c],
            w[pl.ds(pl.multiple_of(c * kc, kc), kc), :],
            preferred_element_type=F32,
        )

        @pl.when(c == 0)
        def _():
            acc[way] = part

        @pl.when(c > 0)
        def _():
            acc[way] = acc[way] + part

    each(lambda c: project(me, c, 0))

    for o, j in pairs:
        for which in range(2):
            kv_copy(o, j, which).wait_recv()
            kv_copy(o, j, which).wait_send()

    def norm_keys(i, carry):
        at = pl.ds(pl.multiple_of(i * BLK, BLK), BLK)
        for h in range(heads):
            lanes = slice(h * DH, (h + 1) * DH)
            khat[at, lanes] = rms_rows(kraw[at, lanes].astype(F32)).astype(BF16)
        return carry

    lax.fori_loop(0, khat.shape[0] // BLK, norm_keys, 0)

    def attend(shard, way):
        for h in range(heads):
            lanes = slice(h * DH, (h + 1) * DH)
            q = acc[way, :, lanes].astype(BF16).astype(F32)
            qh[:, lanes] = (rms_rows(q) * gain[lanes][None]).astype(BF16)
        for a in range(rows // BLK):
            row = mp * bp + shard * (rows // BLK) + a
            flags = [mask[row, mp * bp + b] for b in range(bp)]
            for o, j in pairs:
                owner = lax.rem(mp + patches - o, patches)
                listed = lists[mp, owner, j]
                flag = 0
                for b in range(bp):
                    flag = flag + jnp.where(listed == b, mask[row, owner * bp + b], 0)
                flags.append(flag)
            allowed = jnp.concatenate(
                [jnp.full((1, BLK), flag.astype(F32), F32) for flag in flags], axis=1
            )
            here = pl.ds(a * BLK, BLK)
            there = pl.ds(pl.multiple_of(shard * rows + a * BLK, BLK), BLK)

            def one_head(h, carry):
                lanes = pl.ds(pl.multiple_of(h * DH, DH), DH)
                scores = lax.dot_general(
                    qh[here, lanes], khat[:, lanes], (((1,), (1,)), ((), ())),
                    preferred_element_type=F32,
                )
                weights = (jnp.exp2(scores * SCORE_SCALE) * allowed).astype(BF16)
                values = vall[:, lanes]
                wide = jnp.concatenate([values, jnp.ones_like(values)], axis=1)
                both = jnp.dot(weights, wide, preferred_element_type=F32)
                out[there, lanes] = (both[:, :DH] / both[:, DH:]).astype(BF16)
                return carry

            lax.fori_loop(0, heads, one_head, 0)

    attend(me, 0)

    for h in range(1, n):
        def take(c, h=h):
            for way, shard in ((1, me - h), (0, me + h)):
                @pl.when((shard >= 0) & (shard < n))
                def _(way=way, shard=shard):
                    hop(shard, c, way).wait_recv()

                    @pl.when((me < n - 1) if way == 1 else (me > 0))
                    def _():
                        hop(shard, c, way).start()

                    project(shard, c, way)

        each(take)
        for way, shard in ((1, me - h), (0, me + h)):
            @pl.when((shard >= 0) & (shard < n))
            def _(way=way, shard=shard):
                attend(shard, way)

    for h in range(n):
        for way, shard in ((1, me - h), (0, me + h)):
            @pl.when(
                (shard >= 0) & (shard < n) & ((me < n - 1) if way == 1 else (me > 0))
            )
            def _(way=way, shard=shard):
                each(lambda c: hop(shard, c, way).wait_send())


def body_assisted(
    patches, slots,
    tok, scale, shift, w_hbm, gain, k_hbm, v_hbm, lists, mask, out,
    held, w, w2, acc, qh, qout, qin, kraw, vall, khat, sendkv,
    w_sem, kv_sem, send_sem, recv_sem, ws_sem, wr_sem, qs_sem, qr_sem, kvs_sem, kvr_sem,
):
    me = lax.axis_index("wring")
    mp = lax.axis_index("patch")
    mg = lax.axis_index("grp")
    inner = (me == 1) | (me == 2)
    end = (me == 0) | (me == 3)
    partner = me + 1 - 2 * lax.rem(me, 2)
    cross = 3 - me
    far = 3 - partner
    core = lax.rem(mp, 2)
    side = mp // 2
    rows = tok.shape[0]
    width = tok.shape[1]
    kc = width // CHUNKS
    piece = kc // 8
    heads = gain.shape[0] // DH
    local = k_hbm.shape[0]
    bp = local // BLK

    w_copy = pltpu.make_async_copy(w_hbm, w, w_sem)
    w_copy.start()
    k_copy = pltpu.make_async_copy(k_hbm, kraw.at[pl.ds(0, local)], kv_sem.at[0])
    v_copy = pltpu.make_async_copy(v_hbm, vall.at[pl.ds(0, local)], kv_sem.at[1])
    k_copy.start()
    v_copy.start()

    barrier = pltpu.get_barrier_semaphore()
    pl.semaphore_signal(barrier, inc=1, device_id={"wring": partner})

    @pl.when(inner)
    def _():
        pl.semaphore_signal(barrier, inc=1, device_id={"wring": cross})

    pl.semaphore_signal(barrier, inc=1, device_id={"grp": 1 - mg})
    for o in range(1, patches):
        pl.semaphore_signal(barrier, inc=1, device_id={"patch": lax.rem(mp + o, patches)})
    pl.semaphore_wait(barrier, jnp.where(inner, 1, 0) + 1 + patches)

    def each(fn, count=CHUNKS):
        def one(c, carry):
            fn(c)
            return carry

        lax.fori_loop(0, count, one, 0)

    def spread(stage, c):
        odd = jnp.where(lax.rem(c, 4) == 3, 1, 0)
        even = 1 - odd
        first = core * 4
        count = 1
        where = {"wring": partner}
        if stage in (0, 1):
            first = first + even * (side * 2 + mg) + odd * (mg * 2 + side)
        elif stage == 2:
            first = first + even * (side * 2) + odd * (mg * 2)
            count = 2
        else:
            count = 4
        use_grp = even if stage == 1 else odd
        if stage in (1, 2):
            where = {
                "grp": mg + use_grp * (1 - 2 * mg),
                "patch": mp + (1 - use_grp) * (2 - 4 * side),
            }
        elif stage == 3:
            where = {"patch": mp + 1 - 2 * core}
        at = pl.ds(pl.multiple_of(c * kc + first * piece, piece), count * piece)
        return pltpu.make_async_remote_copy(
            src_ref=(w_hbm if stage == 0 else w2).at[at],
            dst_ref=w2.at[at],
            send_sem=ws_sem.at[stage, c],
            recv_sem=wr_sem.at[stage, c],
            device_id=where,
        )

    @pl.when(end)
    def _():
        each(lambda c: spread(0, c).start())

    step = 16

    def norm_rows(i, carry):
        at = pl.ds(pl.multiple_of(i * step, step), step)
        x = tok[at, :].astype(F32)
        centred = x - jnp.mean(x, axis=-1, keepdims=True)
        spread_of = jnp.mean(centred * centred, axis=-1, keepdims=True)
        y = centred * lax.rsqrt(spread_of + 1e-06) * (1.0 + scale[...][None]) + shift[...][None]
        y = y.astype(BF16)
        for c in range(CHUNKS):
            held[me, c, at, :] = y[:, c * kc : (c + 1) * kc]
        return carry

    lax.fori_loop(0, rows // step, norm_rows, 0)

    def hop(shard, c, target):
        return pltpu.make_async_remote_copy(
            src_ref=held.at[shard, c],
            dst_ref=held.at[shard, c],
            send_sem=send_sem.at[shard, c],
            recv_sem=recv_sem.at[shard, c],
            device_id={"wring": target},
        )

    @pl.when(inner)
    def _():
        for c in range(AHEAD):
            hop(me, c, cross).start()

    k_copy.wait()
    v_copy.wait()

    def kv_copy(o, j, which):
        slot = (o - 1) * slots + j
        return pltpu.make_async_remote_copy(
            src_ref=sendkv.at[slot, which],
            dst_ref=(kraw, vall)[which].at[pl.ds(local + slot * BLK, BLK)],
            send_sem=kvs_sem.at[slot, which],
            recv_sem=kvr_sem.at[slot, which],
            device_id={"patch": lax.rem(mp + o, patches)},
        )

    pairs = [(o, j) for o in range(1, patches) for j in range(slots)]
    for o, j in pairs:
        slot = (o - 1) * slots + j
        picked = jnp.maximum(lists[lax.rem(mp + o, patches), mp, j], 0)
        for which, blocks in enumerate((kraw, vall)):
            chosen = jnp.zeros((BLK, sendkv.shape[3]), F32)
            for b in range(bp):
                chosen = chosen + blocks[b * BLK : (b + 1) * BLK, :].astype(F32) * (
                    jnp.where(picked == b, 1, 0).astype(F32)
                )
            sendkv[slot, which] = chosen.astype(BF16)
        kv_copy(o, j, 0).start()
        kv_copy(o, j, 1).start()

    w_copy.wait()

    def add(slot, c, part):
        @pl.when(c == 0)
        def _():
            acc[slot] = part

        @pl.when(c > 0)
        def _():
            acc[slot] = acc[slot] + part

    def project(shard, c, weight, slot):
        at = pl.ds(pl.multiple_of(c * kc, kc), kc)
        add(slot, c, jnp.dot(held[shard, c], weight[at, :], preferred_element_type=F32))

    def project_two(one, two, c, weight, slot):
        at = pl.ds(pl.multiple_of(c * kc, kc), kc)
        both = jnp.concatenate([held[one, c], held[two, c]], axis=0)
        part = jnp.dot(both, weight[at, :], preferred_element_type=F32)
        add(slot, c, part[:rows])
        add(slot + 1, c, part[rows:])

    def wait_keys():
        for o, j in pairs:
            for which in range(2):
                kv_copy(o, j, which).wait_recv()
                kv_copy(o, j, which).wait_send()

    def norm_keys(i):
        at = pl.ds(pl.multiple_of(i * BLK, BLK), BLK)
        for h in range(heads):
            lanes = slice(h * DH, (h + 1) * DH)
            khat[at, lanes] = rms_rows(kraw[at, lanes].astype(F32)).astype(BF16)

    def norm_queries(read, slot):
        for h in range(heads):
            lanes = slice(h * DH, (h + 1) * DH)
            q = read(lanes).astype(BF16).astype(F32)
            qh[slot, :, lanes] = (rms_rows(q) * gain[lanes][None]).astype(BF16)

    def attend_head(shard, slot, h):
        row = mp * bp + shard
        flags = [mask[row, mp * bp + b] for b in range(bp)]
        for o, j in pairs:
            owner = lax.rem(mp + patches - o, patches)
            listed = lists[mp, owner, j]
            flag = 0
            for b in range(bp):
                flag = flag + jnp.where(listed == b, mask[row, owner * bp + b], 0)
            flags.append(flag)
        allowed = jnp.concatenate(
            [jnp.full((1, BLK), flag.astype(F32), F32) for flag in flags], axis=1
        )
        lanes = pl.ds(pl.multiple_of(h * DH, DH), DH)
        scores = lax.dot_general(
            qh[slot, :, lanes], khat[:, lanes], (((1,), (1,)), ((), ())),
            preferred_element_type=F32,
        )
        weights = (jnp.exp2(scores * SCORE_SCALE) * allowed).astype(BF16)
        values = vall[:, lanes]
        wide = jnp.concatenate([values, jnp.ones_like(values)], axis=1)
        both = jnp.dot(weights, wide, preferred_element_type=F32)
        there = pl.ds(pl.multiple_of(shard * rows, rows), rows)
        out[there, lanes] = (both[:, :DH] / both[:, DH:]).astype(BF16)

    def give(shard):
        return pltpu.make_async_remote_copy(
            src_ref=qout.at[shard],
            dst_ref=qin.at[shard],
            send_sem=qs_sem.at[shard],
            recv_sem=qr_sem.at[shard],
            device_id={"wring": partner},
        )

    @pl.when(inner)
    def _():
        def advance(c):
            @pl.when(c < CHUNKS)
            def _():
                spread(0, c).wait_recv()
                spread(1, c).start()

            @pl.when((c >= 2) & (c < CHUNKS + 2))
            def _():
                spread(1, c - 2).wait_recv()
                spread(2, c - 2).start()

            @pl.when((c >= 4) & (c < CHUNKS + 4))
            def _():
                spread(2, c - 4).wait_recv()
                spread(3, c - 4).start()

        def early(c):
            @pl.when(c + AHEAD < CHUNKS)
            def _():
                hop(me, c + AHEAD, cross).start()

            advance(c)
            hop(cross, c, cross).wait_recv()
            project_two(me, cross, c, w, 0)

            @pl.when(c < bp)
            def _():
                norm_keys(c)

            @pl.when(c == bp + 1)
            def _():
                wait_keys()

            @pl.when(c > bp)
            def _():
                norm_keys(c - 1)

        each(early)

        def middle(c):
            hop(partner, c, cross).wait_recv()
            hop(partner, c, cross).start()

            @pl.when(c == 0)
            def _():
                norm_queries(lambda lanes: acc[0, :, lanes], 0)
                norm_queries(lambda lanes: acc[1, :, lanes], 1)

            project(partner, c, w, 2)

            @pl.when(c < heads)
            def _():
                attend_head(me, 0, c)
                attend_head(cross, 1, c)

        each(middle)
        for c in range(4):
            advance(jnp.int32(c + CHUNKS))

        def borrowed(c):
            spread(3, c).wait_recv()
            project_two(me, cross, c, w2, 3)

        each(borrowed)
        qout[me] = acc[3].astype(BF16)
        give(me).start()
        qout[cross] = acc[4].astype(BF16)
        give(cross).start()
        norm_queries(lambda lanes: acc[2, :, lanes], 0)
        each(lambda h: attend_head(partner, 0, h), heads)

        def late(c):
            hop(far, c, cross).wait_recv()
            project(far, c, w2, 5)
            project(far, c, w, 2)

        each(late)
        qout[far] = acc[5].astype(BF16)
        give(far).start()
        norm_queries(lambda lanes: acc[2, :, lanes], 0)
        each(lambda h: attend_head(far, 0, h), heads)

        def settle(c):
            hop(me, c, cross).wait_send()
            hop(partner, c, cross).wait_send()
            for stage in (1, 2, 3):
                spread(stage, c).wait_send()

        each(settle)
        for shard in (me, cross, far):
            give(shard).wait_send()

    @pl.when(end)
    def _():
        for c in range(CHUNKS - 1):
            spread(0, c).wait_send()
        each(lambda c: hop(me, c, partner).start())
        each(lambda c: project(me, c, w, 0))
        wait_keys()
        each(norm_keys, khat.shape[0] // BLK)
        norm_queries(lambda lanes: acc[0, :, lanes], 0)
        each(lambda h: attend_head(me, 0, h), heads)

        def settle(c):
            hop(me, c, partner).wait_send()

        each(settle)
        spread(0, CHUNKS - 1).wait_send()

        for shard in (partner, far, cross):
            give(shard).wait_recv()
            norm_queries(lambda lanes: qin[shard, :, lanes], 0)
            each(lambda h: attend_head(shard, 0, h), heads)


def on_device(
    n, patches, groups, tokens, mod_scale, mod_shift, q_weight, q_gain, stale_keys,
    stale_values, kv_lists, block_mask
):
    rows, width = tokens.shape
    cols = q_weight.shape[1]
    local = stale_keys.shape[0]
    slots = kv_lists.shape[2]
    got = (patches - 1) * slots
    keys = local + got * BLK
    vmem = pl.BlockSpec(memory_space=pltpu.VMEM)
    smem = pl.BlockSpec(memory_space=pltpu.SMEM)
    hbm = pl.BlockSpec(memory_space=pl.ANY)
    dma = pltpu.SemaphoreType.DMA
    assisted = (
        (n, patches, groups) == (4, 4, 2)
        and rows == BLK
        and cols // DH <= CHUNKS
        and (local // BLK, slots, CHUNKS) == (4, 1, 8)
        and width % (CHUNKS * 8 * 16) == 0
    )
    held = pltpu.VMEM((n, CHUNKS, rows, width // CHUNKS), BF16)
    w = pltpu.VMEM((width, cols), BF16)
    by_key = [pltpu.VMEM((keys, cols), BF16)] * 3 + [pltpu.VMEM((got, 2, BLK, cols), BF16)]
    if assisted:
        kernel = functools.partial(body_assisted, patches, slots)
        scratch = [
            held, w, w,
            pltpu.VMEM((6, rows, cols), F32),
            pltpu.VMEM((2, rows, cols), BF16),
            pltpu.VMEM((n, rows, cols), BF16),
            pltpu.VMEM((n, rows, cols), BF16),
            *by_key,
            dma, dma((2,)),
            dma((n, CHUNKS)), dma((n, CHUNKS)),
            dma((4, CHUNKS)), dma((4, CHUNKS)),
            dma((n,)), dma((n,)),
            dma((got, 2)), dma((got, 2)),
        ]
    else:
        kernel = functools.partial(body, n, patches, slots)
        scratch = [
            held, w,
            pltpu.VMEM((2, rows, cols), F32),
            pltpu.VMEM((rows, cols), BF16),
            *by_key,
            dma, dma((2,)),
            dma((2, n, CHUNKS)), dma((n, CHUNKS)),
            dma((got, 2)), dma((got, 2)),
        ]
    return pl.pallas_call(
        kernel,
        out_shape=jax.ShapeDtypeStruct((local, cols), BF16),
        in_specs=[vmem, vmem, vmem, hbm, vmem, hbm, hbm, smem, smem],
        out_specs=vmem,
        scratch_shapes=scratch,
        compiler_params=pltpu.CompilerParams(
            collective_id=0, has_side_effects=True, vmem_limit_bytes=56 * 1024 * 1024
        ),
    )(
        tokens, mod_scale, mod_shift, q_weight, q_gain, stale_keys,
        stale_values, kv_lists, block_mask,
    )


def solution(mesh):
    placed = (
        P(("grp", "patch", "wring"), None),
        P(),
        P(),
        P(None, "wring"),
        P("wring"),
        P(("grp", "patch"), "wring"),
        P(("grp", "patch"), "wring"),
        P("grp", None, None),
        P("grp", None),
    )
    return jax.shard_map(
        functools.partial(on_device, mesh.shape["wring"], mesh.shape["patch"], mesh.shape["grp"]),
        mesh=mesh,
        in_specs=placed,
        out_specs=P(("grp", "patch"), "wring"),
        check_vma=False,
    )
```

```python
import functools
import math

import jax
import jax.numpy as jnp
from jax import lax
from jax.experimental import pallas as pl
from jax.experimental.pallas import tpu as pltpu
from jax.sharding import PartitionSpec as P

DH = 128
BLK = 128
CHUNKS = 8
AHEAD = 3
F32 = jnp.float32
BF16 = jnp.bfloat16
SCORE_SCALE = math.log2(math.e) / math.sqrt(DH)


def rms_rows(values):
    return values * lax.rsqrt(jnp.mean(values * values, axis=-1, keepdims=True) + 1e-06)


def body(
    n, patches, slots,
    tok, scale, shift, w_hbm, gain, k_hbm, v_hbm, lists, mask, out,
    held, w, acc, qh, kraw, vall, khat, sendkv,
    w_sem, kv_sem, send_sem, recv_sem, kvs_sem, kvr_sem,
):
    me = lax.axis_index("wring")
    mp = lax.axis_index("patch")
    rows = tok.shape[0]
    width = tok.shape[1]
    kc = width // CHUNKS
    heads = gain.shape[0] // DH
    local = k_hbm.shape[0]
    bp = local // BLK

    w_copy = pltpu.make_async_copy(w_hbm, w, w_sem)
    w_copy.start()
    k_copy = pltpu.make_async_copy(k_hbm, kraw.at[pl.ds(0, local)], kv_sem.at[0])
    v_copy = pltpu.make_async_copy(v_hbm, vall.at[pl.ds(0, local)], kv_sem.at[1])
    k_copy.start()
    v_copy.start()

    barrier = pltpu.get_barrier_semaphore()

    @pl.when(me > 0)
    def _():
        pl.semaphore_signal(barrier, inc=1, device_id={"wring": me - 1})

    @pl.when(me < n - 1)
    def _():
        pl.semaphore_signal(barrier, inc=1, device_id={"wring": me + 1})

    for o in range(1, patches):
        pl.semaphore_signal(barrier, inc=1, device_id={"patch": lax.rem(mp + o, patches)})

    step = 16

    def norm_rows(i, carry):
        at = pl.ds(pl.multiple_of(i * step, step), step)
        x = tok[at, :].astype(F32)
        centred = x - jnp.mean(x, axis=-1, keepdims=True)
        spread = jnp.mean(centred * centred, axis=-1, keepdims=True)
        y = centred * lax.rsqrt(spread + 1e-06) * (1.0 + scale[...][None]) + shift[...][None]
        y = y.astype(BF16)
        for c in range(CHUNKS):
            held[me, c, at, :] = y[:, c * kc : (c + 1) * kc]
        return carry

    lax.fori_loop(0, rows // step, norm_rows, 0)

    edges = jnp.where(me > 0, 1, 0) + jnp.where(me < n - 1, 1, 0)
    pl.semaphore_wait(barrier, edges + patches - 1)

    def hop(shard, c, way):
        return pltpu.make_async_remote_copy(
            src_ref=held.at[shard, c],
            dst_ref=held.at[shard, c],
            send_sem=send_sem.at[way, shard, c],
            recv_sem=recv_sem.at[shard, c],
            device_id={"wring": me - 1 if way == 0 else me + 1},
        )

    def each(fn):
        def one(c, carry):
            fn(c)
            return carry

        lax.fori_loop(0, CHUNKS, one, 0)

    def send_own(c):
        @pl.when(me > 0)
        def _():
            hop(me, c, 0).start()

        @pl.when(me < n - 1)
        def _():
            hop(me, c, 1).start()

    each(send_own)

    k_copy.wait()
    v_copy.wait()

    def kv_copy(o, j, which):
        slot = (o - 1) * slots + j
        return pltpu.make_async_remote_copy(
            src_ref=sendkv.at[slot, which],
            dst_ref=(kraw, vall)[which].at[pl.ds(local + slot * BLK, BLK)],
            send_sem=kvs_sem.at[slot, which],
            recv_sem=kvr_sem.at[slot, which],
            device_id={"patch": lax.rem(mp + o, patches)},
        )

    pairs = [(o, j) for o in range(1, patches) for j in range(slots)]
    for o, j in pairs:
        slot = (o - 1) * slots + j
        picked = jnp.maximum(lists[lax.rem(mp + o, patches), mp, j], 0)
        for which, blocks in enumerate((kraw, vall)):
            chosen = jnp.zeros((BLK, sendkv.shape[3]), F32)
            for b in range(bp):
                chosen = chosen + blocks[b * BLK : (b + 1) * BLK, :].astype(F32) * (
                    jnp.where(picked == b, 1, 0).astype(F32)
                )
            sendkv[slot, which] = chosen.astype(BF16)
        kv_copy(o, j, 0).start()
        kv_copy(o, j, 1).start()

    w_copy.wait()

    def project(shard, c, way):
        part = jnp.dot(
            held[shard, c],
            w[pl.ds(pl.multiple_of(c * kc, kc), kc), :],
            preferred_element_type=F32,
        )

        @pl.when(c == 0)
        def _():
            acc[way] = part

        @pl.when(c > 0)
        def _():
            acc[way] = acc[way] + part

    each(lambda c: project(me, c, 0))

    for o, j in pairs:
        for which in range(2):
            kv_copy(o, j, which).wait_recv()
            kv_copy(o, j, which).wait_send()

    def norm_keys(i, carry):
        at = pl.ds(pl.multiple_of(i * BLK, BLK), BLK)
        for h in range(heads):
            lanes = slice(h * DH, (h + 1) * DH)
            khat[at, lanes] = rms_rows(kraw[at, lanes].astype(F32)).astype(BF16)
        return carry

    lax.fori_loop(0, khat.shape[0] // BLK, norm_keys, 0)

    def attend(shard, way):
        for h in range(heads):
            lanes = slice(h * DH, (h + 1) * DH)
            q = acc[way, :, lanes].astype(BF16).astype(F32)
            qh[:, lanes] = (rms_rows(q) * gain[lanes][None]).astype(BF16)
        for a in range(rows // BLK):
            row = mp * bp + shard * (rows // BLK) + a
            flags = [mask[row, mp * bp + b] for b in range(bp)]
            for o, j in pairs:
                owner = lax.rem(mp + patches - o, patches)
                listed = lists[mp, owner, j]
                flag = 0
                for b in range(bp):
                    flag = flag + jnp.where(listed == b, mask[row, owner * bp + b], 0)
                flags.append(flag)
            allowed = jnp.concatenate(
                [jnp.full((1, BLK), flag.astype(F32), F32) for flag in flags], axis=1
            )
            here = pl.ds(a * BLK, BLK)
            there = pl.ds(pl.multiple_of(shard * rows + a * BLK, BLK), BLK)

            def one_head(h, carry):
                lanes = pl.ds(pl.multiple_of(h * DH, DH), DH)
                scores = lax.dot_general(
                    qh[here, lanes], khat[:, lanes], (((1,), (1,)), ((), ())),
                    preferred_element_type=F32,
                )
                weights = (jnp.exp2(scores * SCORE_SCALE) * allowed).astype(BF16)
                values = vall[:, lanes]
                wide = jnp.concatenate([values, jnp.ones_like(values)], axis=1)
                both = jnp.dot(weights, wide, preferred_element_type=F32)
                out[there, lanes] = (both[:, :DH] / both[:, DH:]).astype(BF16)
                return carry

            lax.fori_loop(0, heads, one_head, 0)

    attend(me, 0)

    for h in range(1, n):
        def take(c, h=h):
            for way, shard in ((1, me - h), (0, me + h)):
                @pl.when((shard >= 0) & (shard < n))
                def _(way=way, shard=shard):
                    hop(shard, c, way).wait_recv()

                    @pl.when((me < n - 1) if way == 1 else (me > 0))
                    def _():
                        hop(shard, c, way).start()

                    project(shard, c, way)

        each(take)
        for way, shard in ((1, me - h), (0, me + h)):
            @pl.when((shard >= 0) & (shard < n))
            def _(way=way, shard=shard):
                attend(shard, way)

    for h in range(n):
        for way, shard in ((1, me - h), (0, me + h)):
            @pl.when(
                (shard >= 0) & (shard < n) & ((me < n - 1) if way == 1 else (me > 0))
            )
            def _(way=way, shard=shard):
                each(lambda c: hop(shard, c, way).wait_send())


def body_assisted(
    patches, slots,
    tok, scale, shift, w_hbm, gain, k_hbm, v_hbm, lists, mask, out,
    held, w, w2, acc, qh, qout, qin, kraw, vall, khat, sendkv,
    w_sem, kv_sem, send_sem, recv_sem, ws_sem, wr_sem, qs_sem, qr_sem, kvs_sem, kvr_sem,
):
    me = lax.axis_index("wring")
    mp = lax.axis_index("patch")
    mg = lax.axis_index("grp")
    inner = (me == 1) | (me == 2)
    end = (me == 0) | (me == 3)
    partner = me + 1 - 2 * lax.rem(me, 2)
    cross = 3 - me
    far = 3 - partner
    core = lax.rem(mp, 2)
    side = mp // 2
    rows = tok.shape[0]
    width = tok.shape[1]
    kc = width // CHUNKS
    piece = kc // 8
    heads = gain.shape[0] // DH
    local = k_hbm.shape[0]
    bp = local // BLK

    w_copy = pltpu.make_async_copy(w_hbm, w, w_sem)
    w_copy.start()
    k_copy = pltpu.make_async_copy(k_hbm, kraw.at[pl.ds(0, local)], kv_sem.at[0])
    v_copy = pltpu.make_async_copy(v_hbm, vall.at[pl.ds(0, local)], kv_sem.at[1])
    k_copy.start()
    v_copy.start()

    barrier = pltpu.get_barrier_semaphore()
    pl.semaphore_signal(barrier, inc=1, device_id={"wring": partner})

    @pl.when(inner)
    def _():
        pl.semaphore_signal(barrier, inc=1, device_id={"wring": cross})

    pl.semaphore_signal(barrier, inc=1, device_id={"grp": 1 - mg})
    for o in range(1, patches):
        pl.semaphore_signal(barrier, inc=1, device_id={"patch": lax.rem(mp + o, patches)})
    pl.semaphore_wait(barrier, jnp.where(inner, 1, 0) + 1 + patches)

    def each(fn, count=CHUNKS):
        def one(c, carry):
            fn(c)
            return carry

        lax.fori_loop(0, count, one, 0)

    def spread(stage, c):
        odd = jnp.where(lax.rem(c, 4) == 3, 1, 0)
        even = 1 - odd
        first = core * 4
        count = 1
        where = {"wring": partner}
        if stage in (0, 1):
            first = first + even * (side * 2 + mg) + odd * (mg * 2 + side)
        elif stage == 2:
            first = first + even * (side * 2) + odd * (mg * 2)
            count = 2
        else:
            count = 4
        use_grp = even if stage == 1 else odd
        if stage in (1, 2):
            where = {
                "grp": mg + use_grp * (1 - 2 * mg),
                "patch": mp + (1 - use_grp) * (2 - 4 * side),
            }
        elif stage == 3:
            where = {"patch": mp + 1 - 2 * core}
        at = pl.ds(pl.multiple_of(c * kc + first * piece, piece), count * piece)
        return pltpu.make_async_remote_copy(
            src_ref=(w_hbm if stage == 0 else w2).at[at],
            dst_ref=w2.at[at],
            send_sem=ws_sem.at[stage, c],
            recv_sem=wr_sem.at[stage, c],
            device_id=where,
        )

    @pl.when(end)
    def _():
        each(lambda c: spread(0, c).start())

    step = 16

    def norm_rows(i, carry):
        at = pl.ds(pl.multiple_of(i * step, step), step)
        x = tok[at, :].astype(F32)
        centred = x - jnp.mean(x, axis=-1, keepdims=True)
        spread_of = jnp.mean(centred * centred, axis=-1, keepdims=True)
        y = centred * lax.rsqrt(spread_of + 1e-06) * (1.0 + scale[...][None]) + shift[...][None]
        y = y.astype(BF16)
        for c in range(CHUNKS):
            held[me, c, at, :] = y[:, c * kc : (c + 1) * kc]
        return carry

    lax.fori_loop(0, rows // step, norm_rows, 0)

    def hop(shard, c, target):
        return pltpu.make_async_remote_copy(
            src_ref=held.at[shard, c],
            dst_ref=held.at[shard, c],
            send_sem=send_sem.at[shard, c],
            recv_sem=recv_sem.at[shard, c],
            device_id={"wring": target},
        )

    @pl.when(inner)
    def _():
        for c in range(AHEAD):
            hop(me, c, cross).start()

    k_copy.wait()
    v_copy.wait()

    def kv_copy(o, j, which):
        slot = (o - 1) * slots + j
        return pltpu.make_async_remote_copy(
            src_ref=sendkv.at[slot, which],
            dst_ref=(kraw, vall)[which].at[pl.ds(local + slot * BLK, BLK)],
            send_sem=kvs_sem.at[slot, which],
            recv_sem=kvr_sem.at[slot, which],
            device_id={"patch": lax.rem(mp + o, patches)},
        )

    pairs = [(o, j) for o in range(1, patches) for j in range(slots)]
    for o, j in pairs:
        slot = (o - 1) * slots + j
        picked = jnp.maximum(lists[lax.rem(mp + o, patches), mp, j], 0)
        for which, blocks in enumerate((kraw, vall)):
            chosen = jnp.zeros((BLK, sendkv.shape[3]), F32)
            for b in range(bp):
                chosen = chosen + blocks[b * BLK : (b + 1) * BLK, :].astype(F32) * (
                    jnp.where(picked == b, 1, 0).astype(F32)
                )
            sendkv[slot, which] = chosen.astype(BF16)
        kv_copy(o, j, 0).start()
        kv_copy(o, j, 1).start()

    w_copy.wait()

    def add(slot, c, part):
        @pl.when(c == 0)
        def _():
            acc[slot] = part

        @pl.when(c > 0)
        def _():
            acc[slot] = acc[slot] + part

    def project(shard, c, weight, slot):
        at = pl.ds(pl.multiple_of(c * kc, kc), kc)
        add(slot, c, jnp.dot(held[shard, c], weight[at, :], preferred_element_type=F32))

    def project_two(one, two, c, weight, slot):
        at = pl.ds(pl.multiple_of(c * kc, kc), kc)
        both = jnp.concatenate([held[one, c], held[two, c]], axis=0)
        part = jnp.dot(both, weight[at, :], preferred_element_type=F32)
        add(slot, c, part[:rows])
        add(slot + 1, c, part[rows:])

    def wait_keys():
        for o, j in pairs:
            for which in range(2):
                kv_copy(o, j, which).wait_recv()
                kv_copy(o, j, which).wait_send()

    def norm_keys(i):
        at = pl.ds(pl.multiple_of(i * BLK, BLK), BLK)
        for h in range(heads):
            lanes = slice(h * DH, (h + 1) * DH)
            khat[at, lanes] = rms_rows(kraw[at, lanes].astype(F32)).astype(BF16)

    def norm_queries(read, slot):
        for h in range(heads):
            lanes = slice(h * DH, (h + 1) * DH)
            q = read(lanes).astype(BF16).astype(F32)
            qh[slot, :, lanes] = (rms_rows(q) * gain[lanes][None]).astype(BF16)

    def attend_head(shard, slot, h):
        row = mp * bp + shard
        flags = [mask[row, mp * bp + b] for b in range(bp)]
        for o, j in pairs:
            owner = lax.rem(mp + patches - o, patches)
            listed = lists[mp, owner, j]
            flag = 0
            for b in range(bp):
                flag = flag + jnp.where(listed == b, mask[row, owner * bp + b], 0)
            flags.append(flag)
        allowed = jnp.concatenate(
            [jnp.full((1, BLK), flag.astype(F32), F32) for flag in flags], axis=1
        )
        lanes = pl.ds(pl.multiple_of(h * DH, DH), DH)
        scores = lax.dot_general(
            qh[slot, :, lanes], khat[:, lanes], (((1,), (1,)), ((), ())),
            preferred_element_type=F32,
        )
        weights = (jnp.exp2(scores * SCORE_SCALE) * allowed).astype(BF16)
        values = vall[:, lanes]
        wide = jnp.concatenate([values, jnp.ones_like(values)], axis=1)
        both = jnp.dot(weights, wide, preferred_element_type=F32)
        there = pl.ds(pl.multiple_of(shard * rows, rows), rows)
        out[there, lanes] = (both[:, :DH] / both[:, DH:]).astype(BF16)

    def give(shard):
        return pltpu.make_async_remote_copy(
            src_ref=qout.at[shard],
            dst_ref=qin.at[shard],
            send_sem=qs_sem.at[shard],
            recv_sem=qr_sem.at[shard],
            device_id={"wring": partner},
        )

    @pl.when(inner)
    def _():
        def advance(c):
            @pl.when(c < CHUNKS)
            def _():
                spread(0, c).wait_recv()
                spread(1, c).start()

            @pl.when((c >= 2) & (c < CHUNKS + 2))
            def _():
                spread(1, c - 2).wait_recv()
                spread(2, c - 2).start()

            @pl.when((c >= 4) & (c < CHUNKS + 4))
            def _():
                spread(2, c - 4).wait_recv()
                spread(3, c - 4).start()

        def early(c):
            @pl.when(c + AHEAD < CHUNKS)
            def _():
                hop(me, c + AHEAD, cross).start()

            advance(c)
            hop(cross, c, cross).wait_recv()
            project_two(me, cross, c, w, 0)

            @pl.when(c < bp)
            def _():
                norm_keys(c)

            @pl.when(c == bp + 1)
            def _():
                wait_keys()

            @pl.when(c > bp)
            def _():
                norm_keys(c - 1)

        each(early)

        def middle(c):
            hop(partner, c, cross).wait_recv()
            hop(partner, c, cross).start()

            @pl.when(c == 0)
            def _():
                norm_queries(lambda lanes: acc[0, :, lanes], 0)
                norm_queries(lambda lanes: acc[1, :, lanes], 1)

            project(partner, c, w, 2)

            @pl.when(c < heads)
            def _():
                attend_head(me, 0, c)
                attend_head(cross, 1, c)

        each(middle)
        for c in range(4):
            advance(jnp.int32(c + CHUNKS))

        norm_queries(lambda lanes: acc[2, :, lanes], 0)
        each(lambda h: attend_head(partner, 0, h), heads)

        def borrowed(c):
            spread(3, c).wait_recv()
            project_two(me, cross, c, w2, 3)

        each(borrowed)
        qout[me] = acc[3].astype(BF16)
        give(me).start()
        qout[cross] = acc[4].astype(BF16)
        give(cross).start()

        def late(c):
            hop(far, c, cross).wait_recv()
            project(far, c, w2, 5)

        each(late)
        qout[far] = acc[5].astype(BF16)
        give(far).start()
        each(lambda c: project(far, c, w, 2))
        norm_queries(lambda lanes: acc[2, :, lanes], 0)
        each(lambda h: attend_head(far, 0, h), heads)

        def settle(c):
            hop(me, c, cross).wait_send()
            hop(partner, c, cross).wait_send()
            for stage in (1, 2, 3):
                spread(stage, c).wait_send()

        each(settle)
        for shard in (me, cross, far):
            give(shard).wait_send()

    @pl.when(end)
    def _():
        for c in range(CHUNKS - 1):
            spread(0, c).wait_send()
        each(lambda c: hop(me, c, partner).start())
        each(lambda c: project(me, c, w, 0))
        wait_keys()
        each(norm_keys, khat.shape[0] // BLK)
        norm_queries(lambda lanes: acc[0, :, lanes], 0)
        each(lambda h: attend_head(me, 0, h), heads)

        def settle(c):
            hop(me, c, partner).wait_send()

        each(settle)
        spread(0, CHUNKS - 1).wait_send()

        for shard in (partner, far, cross):
            give(shard).wait_recv()
            norm_queries(lambda lanes: qin[shard, :, lanes], 0)
            each(lambda h: attend_head(shard, 0, h), heads)


def on_device(
    n, patches, groups, tokens, mod_scale, mod_shift, q_weight, q_gain, stale_keys,
    stale_values, kv_lists, block_mask
):
    rows, width = tokens.shape
    cols = q_weight.shape[1]
    local = stale_keys.shape[0]
    slots = kv_lists.shape[2]
    got = (patches - 1) * slots
    keys = local + got * BLK
    vmem = pl.BlockSpec(memory_space=pltpu.VMEM)
    smem = pl.BlockSpec(memory_space=pltpu.SMEM)
    hbm = pl.BlockSpec(memory_space=pl.ANY)
    dma = pltpu.SemaphoreType.DMA
    assisted = (
        (n, patches, groups) == (4, 4, 2)
        and rows == BLK
        and cols // DH <= CHUNKS
        and (local // BLK, slots, CHUNKS) == (4, 1, 8)
        and width % (CHUNKS * 8 * 16) == 0
    )
    held = pltpu.VMEM((n, CHUNKS, rows, width // CHUNKS), BF16)
    w = pltpu.VMEM((width, cols), BF16)
    by_key = [pltpu.VMEM((keys, cols), BF16)] * 3 + [pltpu.VMEM((got, 2, BLK, cols), BF16)]
    if assisted:
        kernel = functools.partial(body_assisted, patches, slots)
        scratch = [
            held, w, w,
            pltpu.VMEM((6, rows, cols), F32),
            pltpu.VMEM((2, rows, cols), BF16),
            pltpu.VMEM((n, rows, cols), BF16),
            pltpu.VMEM((n, rows, cols), BF16),
            *by_key,
            dma, dma((2,)),
            dma((n, CHUNKS)), dma((n, CHUNKS)),
            dma((4, CHUNKS)), dma((4, CHUNKS)),
            dma((n,)), dma((n,)),
            dma((got, 2)), dma((got, 2)),
        ]
    else:
        kernel = functools.partial(body, n, patches, slots)
        scratch = [
            held, w,
            pltpu.VMEM((2, rows, cols), F32),
            pltpu.VMEM((rows, cols), BF16),
            *by_key,
            dma, dma((2,)),
            dma((2, n, CHUNKS)), dma((n, CHUNKS)),
            dma((got, 2)), dma((got, 2)),
        ]
    return pl.pallas_call(
        kernel,
        out_shape=jax.ShapeDtypeStruct((local, cols), BF16),
        in_specs=[vmem, vmem, vmem, hbm, vmem, hbm, hbm, smem, smem],
        out_specs=vmem,
        scratch_shapes=scratch,
        compiler_params=pltpu.CompilerParams(
            collective_id=0, has_side_effects=True, vmem_limit_bytes=56 * 1024 * 1024
        ),
    )(
        tokens, mod_scale, mod_shift, q_weight, q_gain, stale_keys,
        stale_values, kv_lists, block_mask,
    )


def solution(mesh):
    placed = (
        P(("grp", "patch", "wring"), None),
        P(),
        P(),
        P(None, "wring"),
        P("wring"),
        P(("grp", "patch"), "wring"),
        P(("grp", "patch"), "wring"),
        P("grp", None, None),
        P("grp", None),
    )
    return jax.shard_map(
        functools.partial(on_device, mesh.shape["wring"], mesh.shape["patch"], mesh.shape["grp"]),
        mesh=mesh,
        in_specs=placed,
        out_specs=P(("grp", "patch"), "wring"),
        check_vma=False,
    )
```
